32 devices in a mesh: freq: 16 (over z, x, core), cuts: 2 (over y).
Axes of the slice: x: 2, y: 2, z: 4, core: 2. Of those that a mesh axis runs over, the one named last changes fastest.
Arguments:
- wavefield: bfloat16 [16, 2, 2048, 2048], P('freq', None, 'cuts'), may hold values from -6 to 6
- slowness: bfloat16 [16, 2048, 2048], P('freq', 'cuts'), may hold values from 0.25 to 0.546875
- block_inverse: bfloat16 [16, 2, 40, 64, 64], P('freq', None, 'cuts'), may hold values from -0.75 to 0.75
- block_lengths: int32 [16, 40], replicated, may hold values from 1 to 64, 2048 in all within a row
- slab_owner: int32 [1], replicated, may hold values from 0 to 15
- shot_position: int32 [2], replicated, may hold values from 0 to 2047
Outputs:
- image: float32 [1, 2048, 2048], P(None, 'cuts', 'freq')
The draws below stay inside these ranges and needn't reach their ends.
Inputs may be any that keep to these rules, and one draw needn't show every extreme that they name: `block_lengths`: each row lists the lengths of the 40 blocks of a line in order; they sum to 2048 and the longest is exactly 64.
All inputs are finite; a program needn't handle non-finite values.
Results may differ from the reference program's by a relative error of at most 0.012.
Values may be sent and summed in bfloat16 or wider, within the bound.
A program may use at most 128 MiB of HBM per device.

```python
import math
import jax
import jax.numpy as jnp
import numpy as np
from jax import lax

NX = 2048
NY = 2048
B = 64
C = 40
STEPS = 1
FREQS = 16


def shard_levels(stream_key, dims, split, smallest, largest):
    def one(dim, parts):
        heights = jax.random.uniform(jax.random.fold_in(jax.random.fold_in(stream_key, 6), dim), (parts,), jnp.float32, smallest / len(split), largest / len(split))
        return jnp.repeat(jnp.exp(heights), dims[dim] // parts).reshape((-1,) + (1,) * (len(dims) - dim - 1))

    gain = one(*split[0])
    for cut in split[1:]:
        gain = gain * one(*cut)
    return gain


def length_profile(number_of, total, most, lean):
    portions = [(1 << 20) // math.isqrt(standing ** lean) + 1 for standing in range(2, number_of + 1)]
    rest, counts = total - most - (number_of - 1), [1] * (number_of - 1)
    while rest > 0:
        candidates = [i for i in range(number_of - 1) if counts[i] < most]
        mass, left = sum([portions[i] for i in candidates]), rest
        for i in candidates:
            more = min(most - counts[i], max(1, left * portions[i] // mass), rest)
            counts[i] = counts[i] + more
            rest = rest - more
    return np.array([most] + counts)


def uneven(rng, number_of, total, reach, skew):
    if number_of == 2:
        one = jax.random.randint(rng, (), max(1, total - reach), min(reach, total - 1) + 1)
        return jnp.stack([one, total - one])
    lengths = jnp.asarray(length_profile(number_of, total, reach, skew), jnp.int32)
    twos = (number_of - 1) // 2
    donor, sink = lengths[1:1 + 2 * twos:2], lengths[2:2 + 2 * twos:2]
    margin = jnp.minimum(donor - 1, reach - sink)
    passed = jax.random.randint(jax.random.fold_in(rng, 1), (twos,), 0, 1 << 20) % (margin + 1)
    lengths = lengths.at[1:1 + 2 * twos:2].set(donor - passed).at[2:2 + 2 * twos:2].set(sink + passed)
    return lengths[jax.random.permutation(jax.random.fold_in(rng, 2), number_of)]


def bell_draw(own_key, shape, width, bound, split=(), kind=jnp.bfloat16):
    drawn = width * jax.random.normal(own_key, shape, jnp.float32)
    if split:
        drawn = drawn * shard_levels(own_key, shape, split, -0.22, 0.18)
    return jnp.clip(drawn, -bound, bound).astype(kind)


def setup_inputs(seed: int = 0) -> dict:
    splits = jax.random.split(jax.random.key(seed), 7)
    return {
        "wavefield": bell_draw(splits[0], (FREQS, 2, NX, NY), 1.0, 6.0, ((0, 16), (2, 2))),
        "slowness": jnp.clip(0.25 + 0.296875 * jax.random.uniform(splits[1], (FREQS, NX, NY), jnp.float32) ** shard_levels(splits[1], (FREQS, NX, NY), ((0, 16), (1, 2)), -0.2, 0.2), 0.25, 0.546875).astype(jnp.bfloat16),
        "block_inverse": bell_draw(splits[2], (FREQS, 2, C, B, B), 0.05, 0.75, ((0, 16), (2, 2))),
        "block_lengths": jax.vmap(lambda own: uneven(own, C, NY, B, 1))(jax.random.split(splits[3], FREQS)).reshape((FREQS, C)).astype(jnp.int32),
        "slab_owner": jax.random.randint(splits[4], (STEPS,), 0, FREQS).astype(jnp.int32),
        "shot_position": jax.random.randint(splits[5], (2,), 0, min(NX, NY)).astype(jnp.int32),
    }


grid_step = 0.0125
depth_step = 0.02
slow_ref = 0.4
band_low = 5.0
band_width = 55.0
highest = lax.Precision.HIGHEST

def split_length(extent):
    outer_len = 2 ** ((extent.bit_length() - 1) // 2)
    return (outer_len, extent // outer_len)

def outer_table(outer_len, orient):
    first_ids = jnp.arange(outer_len, dtype=jnp.int32)
    indices = first_ids[:, None] * first_ids[None, :] % outer_len
    angles = orient * 2.0 * math.pi / outer_len * indices.astype(jnp.float32)
    cosine = jnp.cos(angles) / math.sqrt(outer_len)
    sine = jnp.sin(angles) / math.sqrt(outer_len)
    first = jnp.stack([cosine, sine], axis=1)
    second = jnp.stack([-sine, cosine], axis=1)
    return jnp.stack([first, second], axis=0).astype(jnp.bfloat16)

def inner_table(outer_len, inner_len, orient):
    extent = outer_len * inner_len
    outer_ids = jnp.arange(outer_len, dtype=jnp.int32)[:, None, None]
    inner_ids = jnp.arange(inner_len, dtype=jnp.int32)[None, :, None]
    freq_ids = jnp.arange(inner_len, dtype=jnp.int32)[None, None, :]
    indices = inner_ids * (outer_ids + outer_len * freq_ids) % extent
    angles = orient * 2.0 * math.pi / extent * indices.astype(jnp.float32)
    cosine = jnp.cos(angles) / math.sqrt(inner_len)
    sine = jnp.sin(angles) / math.sqrt(inner_len)
    first = jnp.stack([cosine, sine], axis=2)
    second = jnp.stack([-sine, cosine], axis=2)
    return jnp.stack([first, second], axis=2).astype(jnp.bfloat16)

def mixing(formula, operand, table):
    return jnp.einsum(formula, operand.astype(jnp.float32), table.astype(jnp.float32), precision=highest)

def forward_lines(field):
    rows = field.shape[1]
    outer_len, inner_len = split_length(field.shape[2])
    shaped = field.reshape(2, rows, outer_len, inner_len)
    first_section = mixing('cmab,cadk->mbdk', shaped, outer_table(outer_len, -1.0)).astype(jnp.bfloat16)
    return mixing('mbdk,kbdeq->kmeq', first_section, inner_table(outer_len, inner_len, -1.0)).astype(jnp.bfloat16)

def across_forward(columns):
    count_k, extent_x, _, count_q = columns.shape
    outer_len, inner_len = split_length(extent_x)
    shaped = columns.reshape(count_k, outer_len, inner_len, 2, count_q)
    first_section = mixing('kabcq,cadz->kbqdz', shaped, outer_table(outer_len, -1.0)).astype(jnp.bfloat16)
    return mixing('kbqdz,zbdwu->zkqwu', first_section, inner_table(outer_len, inner_len, -1.0))

def across_inverse(spectrum, extent_x):
    count_k = spectrum.shape[1]
    count_q = spectrum.shape[2]
    outer_len, inner_len = split_length(extent_x)
    first_section = mixing('zkqwu,zbwdu->zkqdb', spectrum, inner_table(outer_len, inner_len, 1.0)).astype(jnp.bfloat16)
    second_section = mixing('zkqdb,daez->kabeq', first_section, outer_table(outer_len, 1.0)).astype(jnp.bfloat16)
    return second_section.reshape(count_k, extent_x, 2, count_q)

def lines_inverse(spectrum, extent_y):
    rows = spectrum.shape[1]
    outer_len, inner_len = split_length(extent_y)
    first_section = mixing('kmdq,kbdeq->kmeb', spectrum, inner_table(outer_len, inner_len, 1.0)).astype(jnp.bfloat16)
    second_section = mixing('kmeb,eack->cmab', first_section, outer_table(outer_len, 1.0))
    return second_section.reshape(2, rows, extent_y)

def wave_numbers(indices, extent):
    signed = jnp.where(indices < extent // 2, indices, indices - extent)
    return signed.astype(jnp.float32) * (2.0 * math.pi / (extent * grid_step))

def propagator(angular, k_start, k_count, extent_x, extent_y):
    outer_x, inner_x = split_length(extent_x)
    outer_y, inner_y = split_length(extent_y)
    cross_ids = jnp.arange(outer_x, dtype=jnp.int32)[:, None] + outer_x * jnp.arange(inner_x, dtype=jnp.int32)[None, :]
    line_ids = (k_start + jnp.arange(k_count, dtype=jnp.int32))[:, None] + outer_y * jnp.arange(inner_y, dtype=jnp.int32)[None, :]
    wave_x = wave_numbers(cross_ids, extent_x)
    wave_y = wave_numbers(line_ids, extent_y)
    vertical = (angular * slow_ref) ** 2 - wave_x[:, None, None, :] ** 2 - wave_y[None, :, :, None] ** 2
    root_abs = jnp.sqrt(jnp.abs(vertical))
    real_part = jnp.where(vertical > 0, jnp.cos(root_abs * depth_step), jnp.exp(-root_abs * depth_step))
    imag_part = jnp.where(vertical > 0, jnp.sin(root_abs * depth_step), jnp.zeros_like(root_abs))
    return (real_part, imag_part)

def shift_phase(kspace, prop_re, prop_im):
    real_in = kspace[:, :, :, 0, :]
    imag_in = kspace[:, :, :, 1, :]
    real_out = real_in * prop_re - imag_in * prop_im
    imag_out = real_in * prop_im + imag_in * prop_re
    return jnp.stack([real_out, imag_out], axis=3).astype(jnp.bfloat16)

def block_correction(turned, matrices, block_len, extent_y):
    block_count = matrices.shape[1]
    capacity = matrices.shape[2]
    starts = (jnp.cumsum(block_len) - block_len).astype(jnp.int32)
    offsets = jnp.arange(capacity, dtype=jnp.int32)
    source = jnp.minimum(starts[:, None] + offsets[None, :], extent_y - 1).reshape(-1).astype(jnp.int32)
    occupied = (offsets[None, :] < block_len[:, None]).reshape(-1)

    def slotted(part):
        picked = jnp.take(part.astype(jnp.float32), source, axis=1)
        picked = jnp.where(occupied[None, :], picked, jnp.zeros_like(picked))
        return picked.reshape(part.shape[0], block_count, capacity)
    slot_re = slotted(turned[0])
    slot_im = slotted(turned[1])
    mat_re = matrices[0].astype(jnp.float32)
    mat_im = matrices[1].astype(jnp.float32)

    def product(first_op, second_op):
        return jnp.einsum('rcj,cij->rci', first_op, second_op, precision=highest)
    out_re = product(slot_re, mat_re) - product(slot_im, mat_im)
    out_im = product(slot_re, mat_im) + product(slot_im, mat_re)
    cell_ids = jnp.arange(extent_y, dtype=jnp.int32)
    block_end = starts + block_len
    shift_sum = lax.optimization_barrier(jnp.sum(jnp.where(block_end[None, :] <= cell_ids[:, None], capacity - block_len[None, :], 0), axis=1))
    position = (cell_ids + shift_sum).astype(jnp.int32)
    back_re = jnp.take(out_re.reshape(out_re.shape[0], -1), position, axis=1)
    back_im = jnp.take(out_im.reshape(out_im.shape[0], -1), position, axis=1)
    return (back_re, back_im)

def image_phase(angular, shot_position, depth_index):
    offset_x = (jnp.arange(NX, dtype=jnp.int32) - shot_position[0]).astype(jnp.float32) * grid_step
    offset_y = (jnp.arange(NY, dtype=jnp.int32) - shot_position[1]).astype(jnp.float32) * grid_step
    depth_now = (depth_index + 1) * depth_step
    distance = jnp.sqrt(offset_x[:, None] ** 2 + offset_y[None, :] ** 2 + depth_now * depth_now)
    return angular * slow_ref * distance

def reference(wavefield, slowness, block_inverse, block_lengths, slab_owner, shot_position):
    outer_y, inner_y = split_length(NY)

    def one_freq(carry, inputs):
        freq_index, current = inputs
        angular = 2.0 * math.pi * (band_low + band_width * (freq_index.astype(jnp.float32) + 0.5) / FREQS)
        prop_re, prop_im = propagator(angular, 0, outer_y, NX, NY)
        image_parts = []
        for depth_index in range(STEPS):
            owner_id = slab_owner[depth_index]
            slab_now = lax.dynamic_index_in_dim(slowness, owner_id, 0, keepdims=False).astype(jnp.float32)
            matrices = lax.dynamic_index_in_dim(block_inverse, owner_id, 0, keepdims=False)
            block_len = lax.dynamic_index_in_dim(block_lengths, owner_id, 0, keepdims=False)
            spectrum = forward_lines(current)
            kspace = across_forward(spectrum)
            shifted = shift_phase(kspace, prop_re, prop_im)
            restored = across_inverse(shifted, NX)
            spatial = lines_inverse(restored, NY)
            phases = angular * depth_step * (slab_now - slow_ref)
            cos_part = jnp.cos(phases)
            sin_part = jnp.sin(phases)
            turned = ((spatial[0] * cos_part - spatial[1] * sin_part).astype(jnp.bfloat16), (spatial[0] * sin_part + spatial[1] * cos_part).astype(jnp.bfloat16))
            correction = block_correction(turned, matrices, block_len, NY)
            values_re = turned[0].astype(jnp.float32) + correction[0]
            values_im = turned[1].astype(jnp.float32) + correction[1]
            angle_img = image_phase(angular, shot_position, depth_index)
            image_parts.append((values_re * jnp.cos(angle_img) - values_im * jnp.sin(angle_img)) / math.sqrt(FREQS))
            current = jnp.stack([values_re, values_im]).astype(jnp.bfloat16)
        return (carry + jnp.stack(image_parts), None)
    start_image = jnp.zeros((STEPS, NX, NY), jnp.float32)
    image, _ = lax.scan(one_freq, start_image, (jnp.arange(FREQS, dtype=jnp.int32), wavefield))
    return image
```

```python
import functools
import math

import jax
import jax.numpy as jnp
import numpy as np
from jax import lax
from jax.experimental import pallas as pl
from jax.experimental.pallas import tpu as pltpu
from jax.sharding import PartitionSpec as P

grid_step = 0.0125
depth_step = 0.02
slow_ref = 0.4
band_low = 5.0
band_width = 55.0

RADIX = 8
SUB = 16
LANE = 128
PAD = 128
VMEM_LIMIT = 56 * 1024 * 1024
BF = jnp.bfloat16
F32 = jnp.float32


def fit(fn, top, degree):
    cheb = np.polynomial.chebyshev.Chebyshev.interpolate(fn, degree, domain=[0.0, top])
    return [float(c) for c in cheb.convert(kind=np.polynomial.Polynomial).coef]


def root_cos(w):
    return np.cos(np.sqrt(np.maximum(w, 0.0)))


def root_sinc(w):
    return np.sinc(np.sqrt(np.maximum(w, 0.0)) / np.pi)


COS_WIDE = fit(root_cos, 10.0, 7)
SINC_WIDE = fit(root_sinc, 10.0, 6)
COS_SLIM = fit(root_cos, 1.6, 4)
SINC_SLIM = fit(root_sinc, 1.6, 4)


def horner(coefs, x):
    acc = jnp.full_like(x, coefs[-1])
    for c in coefs[-2::-1]:
        acc = acc * x + c
    return acc


def fourier_tables(extent):
    inner = extent // RADIX
    k = np.arange(RADIX)[:, None, None]
    q = np.arange(inner)[None, :, None]
    b = np.arange(inner)[None, None, :]
    angle = 2.0 * np.pi / extent * ((b * (k + RADIX * q)) % extent)
    cosine = np.cos(angle) / math.sqrt(extent)
    sine = np.sin(angle) / math.sqrt(extent)
    top = np.concatenate([cosine, sine], axis=2)
    low = np.concatenate([-sine, cosine], axis=2)
    table = np.concatenate([top, low], axis=1).astype(np.float32)
    return table.astype(BF), np.ascontiguousarray(table.transpose(0, 2, 1)).astype(BF)


def radix8(parts, sign):
    def add(x, y):
        return (x[0] + y[0], x[1] + y[1])

    def sub(x, y):
        return (x[0] - y[0], x[1] - y[1])

    def turn(x):
        return (x[1], -x[0]) if sign < 0 else (-x[1], x[0])

    half = math.sqrt(0.5)

    def four(x0, x1, x2, x3):
        t0, t1, t2, t3 = add(x0, x2), sub(x0, x2), add(x1, x3), turn(sub(x1, x3))
        return [add(t0, t2), add(t1, t3), sub(t0, t2), sub(t1, t3)]

    even = four(parts[0], parts[2], parts[4], parts[6])
    odd = four(parts[1], parts[3], parts[5], parts[7])
    turned1 = turn(odd[1])
    turned3 = turn(odd[3])
    odd[1] = ((odd[1][0] + turned1[0]) * half, (odd[1][1] + turned1[1]) * half)
    odd[2] = turn(odd[2])
    odd[3] = ((turned3[0] - odd[3][0]) * half, (turned3[1] - odd[3][1]) * half)
    return [add(even[i], odd[i]) for i in range(4)] + [sub(even[i], odd[i]) for i in range(4)]


def rows_of(step):
    return pl.ds(pl.multiple_of(step * SUB, SUB), SUB)


def residue(cut, shift, chunk, cuts, per):
    return lax.rem(cut + (cuts - shift), cuts) * per + chunk


def lines_kernel(cuts, cut_ref, p_ref, ft_ref, *rest):
    outs, y1 = rest[:-1], rest[-1]
    rows, extent = p_ref.shape[1], p_ref.shape[2]
    inner = extent // RADIX
    per = RADIX // cuts

    @pl.loop(0, rows // SUB)
    def _(step):
        at = rows_of(step)
        for l in range(0, inner, LANE):
            parts = [
                (
                    p_ref[0, at, a * inner + l : a * inner + l + LANE].astype(F32),
                    p_ref[1, at, a * inner + l : a * inner + l + LANE].astype(F32),
                )
                for a in range(RADIX)
            ]
            for k, (re, im) in enumerate(radix8(parts, -1)):
                y1[k, at, l : l + LANE] = re.astype(BF)
                y1[k, at, inner + l : inner + l + LANE] = im.astype(BF)

    cut = cut_ref[0]
    for s in range(cuts):
        for c in range(per):
            k = residue(cut, s, c, cuts, per)
            outs[s * per + c][...] = jnp.dot(y1[k], ft_ref[k], preferred_element_type=F32).astype(BF)


def across_kernel(cuts, *refs):
    pieces = refs[:cuts]
    f_ref, ft_ref, wx_ref, wy_ref = refs[cuts : cuts + 4]
    outs = refs[cuts + 4 : -3]
    y1, z, kb = refs[-3:]
    rows = pieces[0].shape[0]
    inner = rows * cuts // RADIX
    width = pieces[0].shape[1] // 2

    @pl.loop(0, inner // SUB)
    def _(step):
        for l in range(0, width, LANE):
            parts = []
            for a in range(RADIX):
                piece = pieces[a * inner // rows]
                at = pl.ds(pl.multiple_of(a * inner % rows + step * SUB, SUB), SUB)
                parts.append(
                    (
                        piece[at, l : l + LANE].astype(F32),
                        piece[at, width + l : width + l + LANE].astype(F32),
                    )
                )
            low = pl.ds(pl.multiple_of(step * SUB, SUB), SUB)
            high = pl.ds(pl.multiple_of(inner + step * SUB, SUB), SUB)
            for k, (re, im) in enumerate(radix8(parts, -1)):
                y1[k, low, l : l + LANE] = re.astype(BF)
                y1[k, high, l : l + LANE] = im.astype(BF)

    @pl.loop(0, RADIX)
    def _(k):
        z[...] = jnp.dot(f_ref[k], y1[k], preferred_element_type=F32)

        @pl.loop(0, inner // SUB)
        def _(step):
            low = pl.ds(pl.multiple_of(step * SUB, SUB), SUB)
            high = pl.ds(pl.multiple_of(inner + step * SUB, SUB), SUB)
            w = wx_ref[k, low, :] - wy_ref[...]
            size = jnp.abs(w)
            root = size * lax.rsqrt(jnp.maximum(size, 1e-30))
            onward = w > 0
            re = jnp.where(onward, horner(COS_WIDE, w), jnp.exp(-root))
            im = jnp.where(onward, root * horner(SINC_WIDE, w), 0.0)
            zr, zi = z[low, :], z[high, :]
            kb[low, :] = (zr * re - zi * im).astype(BF)
            kb[high, :] = (zr * im + zi * re).astype(BF)

        y1[k] = jnp.dot(ft_ref[k], kb[...], preferred_element_type=F32).astype(BF)

    @pl.loop(0, inner // SUB)
    def _(step):
        low = pl.ds(pl.multiple_of(step * SUB, SUB), SUB)
        high = pl.ds(pl.multiple_of(inner + step * SUB, SUB), SUB)
        for l in range(0, width, LANE):
            parts = [
                (y1[k, low, l : l + LANE].astype(F32), y1[k, high, l : l + LANE].astype(F32))
                for k in range(RADIX)
            ]
            for a, (re, im) in enumerate(radix8(parts, 1)):
                outs[a][low, l : l + LANE] = re.astype(BF)
                outs[a][low, width + l : width + l + LANE] = im.astype(BF)


def band_kernel(g_ref, off_ref, out_ref):
    rows, lanes = g_ref.shape[1], g_ref.shape[2]
    width = out_ref.shape[3]
    offset = off_ref[...]
    for part in range(2):
        x = jnp.concatenate(
            [g_ref[part].astype(F32), jnp.zeros((rows, width - lanes), F32)], axis=1
        )
        bit = 1
        while bit < width:
            x = jnp.where((offset & bit) != 0, pltpu.roll(x, bit, 1), x)
            bit *= 2
        out_ref[part, 0] = x.astype(BF)


def finish_kernel(cuts, split, cut_ref, num_ref, *refs):
    pieces = refs[:RADIX]
    f_ref, slow_in, band_ref, dx_ref, dy_ref, out_ref, z1, u, cr, ci = refs[RADIX:]
    rows, extent = slow_in.shape
    inner = extent // RADIX
    per = RADIX // cuts
    cut = cut_ref[0]
    scale = num_ref[0]
    turns = num_ref[1]
    share = num_ref[2]
    for s in range(cuts):
        for c in range(per):
            k = residue(cut, s, c, cuts, per)
            z1[k] = jnp.dot(
                pieces[s * per + c][...], f_ref[k], preferred_element_type=F32
            ).astype(BF)
    u[:, :, :PAD] = jnp.zeros((2, rows, PAD), BF)
    u[:, :, PAD + extent :] = jnp.zeros((2, rows, PAD), BF)

    @pl.loop(0, rows // SUB)
    def _(step):
        at = rows_of(step)
        for l in range(0, inner, LANE):
            parts = [
                (
                    z1[k, at, l : l + LANE].astype(F32),
                    z1[k, at, inner + l : inner + l + LANE].astype(F32),
                )
                for k in range(RADIX)
            ]
            for a, (re, im) in enumerate(radix8(parts, 1)):
                at_y = a * inner + l
                theta = scale * (slow_in[at, at_y : at_y + LANE].astype(F32) - slow_ref)
                square = theta * theta
                cosine = horner(COS_SLIM, square)
                sine = theta * horner(SINC_SLIM, square)
                u[0, at, PAD + at_y : PAD + at_y + LANE] = (re * cosine - im * sine).astype(BF)
                u[1, at, PAD + at_y : PAD + at_y + LANE] = (re * sine + im * cosine).astype(BF)

    contract = (((1,), (1,)), ((), ()))

    def mul(x, y):
        return lax.dot_general(x, y, contract, preferred_element_type=F32)

    for t in range(RADIX):
        wr = u[0, :, t * inner : t * inner + inner + 2 * PAD]
        wi = u[1, :, t * inner : t * inner + inner + 2 * PAD]
        cr[...] = mul(wr, band_ref[0, t]) - mul(wi, band_ref[1, t])
        ci[...] = mul(wr, band_ref[1, t]) + mul(wi, band_ref[0, t])

        @pl.loop(0, rows // SUB)
        def _(step):
            at = rows_of(step)
            first = t * inner
            vr = u[0, at, PAD + first : PAD + first + inner].astype(F32) + cr[at, :]
            vi = u[1, at, PAD + first : PAD + first + inner].astype(F32) + ci[at, :]
            distance = jnp.sqrt(dx_ref[at, :] + dy_ref[:, first : first + inner])
            turn = turns * distance
            theta = (turn - jnp.floor(turn + 0.5)) * (2.0 * math.pi)
            square = theta * theta
            value = (
                vr * horner(COS_WIDE, square) - vi * (theta * horner(SINC_WIDE, square))
            ) * share
            if split:
                size = out_ref.shape[2]
                for e in range(0, inner, size):
                    out_ref[(first + e) // size, at, :] = value[:, e : e + size]
            else:
                out_ref[at, first : first + inner] = value


def params():
    return pltpu.CompilerParams(vmem_limit_bytes=VMEM_LIMIT)


VMEM = pl.BlockSpec(memory_space=pltpu.VMEM)
SMEM = pl.BlockSpec(memory_space=pltpu.SMEM)


def lines_forward(field, ft, cut, cuts):
    rows, extent = field.shape[1], field.shape[2]
    inner = extent // RADIX
    tile = math.gcd(rows, 256)
    return pl.pallas_call(
        functools.partial(lines_kernel, cuts),
        grid=(rows // tile,),
        out_shape=[jax.ShapeDtypeStruct((rows, 2 * inner), BF)] * RADIX,
        in_specs=[
            SMEM,
            pl.BlockSpec((2, tile, extent), lambda i: (0, i, 0)),
            pl.BlockSpec(ft.shape, lambda i: (0, 0, 0)),
        ],
        out_specs=[pl.BlockSpec((tile, 2 * inner), lambda i: (i, 0))] * RADIX,
        scratch_shapes=[pltpu.VMEM((RADIX, tile, 2 * inner), BF)],
        compiler_params=params(),
        cost_estimate=pl.CostEstimate(
            flops=rows * RADIX * (2 * inner) ** 2 * 2,
            bytes_accessed=rows * extent * 8 + ft.size * 2,
            transcendentals=0,
        ),
        name="lines_forward",
    )(cut, field, ft)


def across(pieces, f, ft, wx, wy, cuts):
    rows = pieces[0].shape[0]
    inner = rows * cuts // RADIX
    width = pieces[0].shape[1] // 2
    return pl.pallas_call(
        functools.partial(across_kernel, cuts),
        out_shape=[jax.ShapeDtypeStruct((inner, 2 * width), BF)] * RADIX,
        in_specs=[VMEM] * (cuts + 4),
        out_specs=[VMEM] * RADIX,
        scratch_shapes=[
            pltpu.VMEM((RADIX, 2 * inner, width), BF),
            pltpu.VMEM((2 * inner, width), F32),
            pltpu.VMEM((2 * inner, width), BF),
        ],
        compiler_params=params(),
        cost_estimate=pl.CostEstimate(
            flops=2 * width * RADIX * (2 * inner) ** 2 * 2,
            bytes_accessed=24 * 1024 * 1024,
            transcendentals=0,
        ),
        name="across",
    )(*pieces, f, ft, wx, wy)


def band(rows_g, offsets, inner):
    extent = rows_g.shape[1]
    return pl.pallas_call(
        band_kernel,
        grid=(RADIX,),
        out_shape=jax.ShapeDtypeStruct((2, RADIX, inner, inner + 2 * PAD), BF),
        in_specs=[
            pl.BlockSpec((2, inner, rows_g.shape[2]), lambda t: (0, t, 0)),
            pl.BlockSpec((inner, 1), lambda t: (t, 0)),
        ],
        out_specs=pl.BlockSpec((2, 1, inner, inner + 2 * PAD), lambda t: (0, t, 0, 0)),
        compiler_params=params(),
        cost_estimate=pl.CostEstimate(
            flops=0, bytes_accessed=40 * 1024 * 1024, transcendentals=0
        ),
        name="band",
    )(rows_g, offsets)


def finish(pieces, chunk, f, slab, bands, dx, dy, cut, numbers, cuts, freqs):
    rows = pieces[0].shape[0]
    extent = slab.shape[1]
    inner = extent // RADIX
    size = extent // freqs
    split = size % LANE == 0 and inner % size == 0
    tile = math.gcd(rows, 128)
    steps = rows // tile
    if split:
        out_shape = jax.ShapeDtypeStruct((freqs, rows, size), F32)
        out_spec = pl.BlockSpec((freqs, tile, size), lambda i: (0, i, 0))
    else:
        out_shape = jax.ShapeDtypeStruct((rows, extent), F32)
        out_spec = pl.BlockSpec((tile, extent), lambda i: (i, 0))
    return pl.pallas_call(
        functools.partial(finish_kernel, cuts, split),
        grid=(steps,),
        out_shape=out_shape,
        in_specs=[SMEM, SMEM]
        + [pl.BlockSpec((tile, 2 * inner), lambda i: (i, 0))] * RADIX
        + [
            pl.BlockSpec(f.shape, lambda i: (0, 0, 0)),
            pl.BlockSpec((tile, extent), lambda i: (i + chunk * steps, 0)),
            pl.BlockSpec(bands.shape, lambda i: (0, 0, 0, 0)),
            pl.BlockSpec((tile, 1), lambda i: (i + chunk * steps, 0)),
            pl.BlockSpec((1, extent), lambda i: (0, 0)),
        ],
        out_specs=out_spec,
        scratch_shapes=[
            pltpu.VMEM((RADIX, tile, 2 * inner), BF),
            pltpu.VMEM((2, tile, extent + 2 * PAD), BF),
            pltpu.VMEM((tile, inner), F32),
            pltpu.VMEM((tile, inner), F32),
        ],
        compiler_params=params(),
        cost_estimate=pl.CostEstimate(
            flops=rows * RADIX * (2 * inner) ** 2 * 6,
            bytes_accessed=32 * 1024 * 1024,
            transcendentals=0,
        ),
        name="finish",
    )(cut, numbers, *pieces, f, slab, bands, dx, dy), split


def wave_numbers(indices, extent):
    signed = jnp.where(indices < extent // 2, indices, indices - extent)
    return signed.astype(F32) * (2.0 * math.pi / (extent * grid_step))


def back(x, axis, shift):
    count = lax.axis_size(axis)
    return lax.ppermute(x, axis, [(i, (i - shift) % count) for i in range(count)])


def forth(x, axis, shift):
    count = lax.axis_size(axis)
    return lax.ppermute(x, axis, [(i, (i + shift) % count) for i in range(count)])


def body(wavefield, slowness, block_inverse, block_lengths, slab_owner, shot_position):
    cuts = lax.axis_size("cuts")
    freqs = lax.axis_size("freq")
    rows, extent_y = wavefield.shape[2], wavefield.shape[3]
    extent_x = rows * cuts
    inner_x, inner_y = extent_x // RADIX, extent_y // RADIX
    per = RADIX // cuts
    freq_index = lax.axis_index("freq")
    cut_index = lax.axis_index("cuts")
    cut = jnp.reshape(cut_index, (1,)).astype(jnp.int32)
    hertz = band_low + band_width * (freq_index.astype(F32) + 0.5) / freqs
    angular = 2.0 * math.pi * hertz

    fy, fty = fourier_tables(extent_y)
    fy, fty = jnp.asarray(fy), jnp.asarray(fty)
    if extent_x == extent_y:
        fx, ftx = fy, fty
    else:
        fx, ftx = fourier_tables(extent_x)
        fx, ftx = jnp.asarray(fx), jnp.asarray(ftx)

    owner = slab_owner[0]
    mine = freq_index == owner
    operators = lax.psum(jnp.where(mine, block_inverse[0], jnp.zeros_like(block_inverse[0])), "freq")
    slab = lax.psum(jnp.where(mine, slowness[0], jnp.zeros_like(slowness[0])), "freq")

    spectrum = lines_forward(wavefield[0], fty, cut, cuts)

    count_x = jnp.arange(RADIX, dtype=jnp.int32)[:, None] + RADIX * jnp.arange(inner_x, dtype=jnp.int32)[None, :]
    wx = (depth_step * depth_step) * (
        (angular * slow_ref) ** 2 - wave_numbers(count_x, extent_x) ** 2
    )
    wx = wx[:, :, None]
    received = [[None] * cuts for _ in range(per)]
    for c in range(per):
        received[c][0] = spectrum[c]
        for s in range(1, cuts):
            received[c][s] = back(spectrum[s * per + c], "cuts", s)
    results = []
    for c in range(per):
        line = cut_index * per + c + RADIX * jnp.arange(inner_y, dtype=jnp.int32)
        wy = ((depth_step * depth_step) * wave_numbers(line, extent_y) ** 2)[None, :]
        results.append(across(received[c], fx, ftx, wx, wy, cuts))

    whole = [operators]
    for s in range(1, cuts):
        whole.append(back(operators, "cuts", s))
    stacked = jnp.stack(whole)
    stacked = jnp.take(stacked, (jnp.arange(cuts) - cut_index) % cuts, axis=0)
    capacity = stacked.shape[-1]
    blocks = stacked.shape[2] * cuts
    matrices = jnp.moveaxis(stacked, 0, 1).reshape(2, blocks * capacity, capacity)
    lengths = lax.dynamic_index_in_dim(block_lengths, owner, 0, keepdims=False)
    ends = jnp.cumsum(lengths)
    starts = ends - lengths
    cells = jnp.arange(extent_y, dtype=jnp.int32)
    which = jnp.sum((ends[None, :] <= cells[:, None]).astype(jnp.int32), axis=1)
    chosen = which[:, None] == jnp.arange(blocks, dtype=jnp.int32)[None, :]
    start = jnp.sum(jnp.where(chosen, starts[None, :], 0), axis=1)
    length = jnp.sum(jnp.where(chosen, lengths[None, :], 0), axis=1)
    slot = which * capacity + cells - start
    picked = jnp.take(matrices, slot, axis=1)
    picked = jnp.where(
        jnp.arange(capacity, dtype=jnp.int32)[None, None, :] < length[None, :, None], picked, 0
    ).astype(BF)
    picked = jnp.pad(picked, ((0, 0), (0, 0), (0, -capacity % LANE)))
    offsets = start - (cells // inner_y * inner_y - PAD)
    bands = band(picked, offsets[:, None].astype(jnp.int32), inner_y)

    rows_x = cut_index * rows + jnp.arange(rows, dtype=jnp.int32)
    dx = (((rows_x - shot_position[0]).astype(F32) * grid_step) ** 2)[:, None]
    dy = (((cells - shot_position[1]).astype(F32) * grid_step) ** 2 + depth_step * depth_step)[None, :]
    numbers = jnp.stack(
        [angular * depth_step, hertz * slow_ref, jnp.asarray(1.0 / math.sqrt(freqs), F32)]
    )

    chunks = rows // inner_x
    images = []
    for h in range(chunks):
        pieces = []
        for s in range(cuts):
            for c in range(per):
                x = results[c][s * chunks + h]
                pieces.append(x if s == 0 else forth(x, "cuts", s))
        part, split = finish(pieces, h, fy, slab, bands, dx, dy, cut, numbers, cuts, freqs)
        if split:
            part = lax.psum_scatter(part, "freq", scatter_dimension=0, tiled=False)
        else:
            part = lax.psum_scatter(part, "freq", scatter_dimension=1, tiled=True)
        images.append(part)
    return jnp.concatenate(images, axis=0)[None]


def solution(mesh):
    placed = (
        P("freq", None, "cuts", None),
        P("freq", "cuts", None),
        P("freq", None, "cuts", None, None),
        P(),
        P(),
        P(),
    )
    return jax.shard_map(
        body, mesh=mesh, in_specs=placed, out_specs=P(None, "cuts", "freq"), check_vma=False
    )
```

```python
import functools
import math

import jax
import jax.numpy as jnp
import numpy as np
from jax import lax
from jax.experimental import pallas as pl
from jax.experimental.pallas import tpu as pltpu
from jax.sharding import PartitionSpec as P

grid_step = 0.0125
depth_step = 0.02
slow_ref = 0.4
band_low = 5.0
band_width = 55.0

RADIX = 8
SUB = 16
LANE = 128
PAD = 128
VMEM_LIMIT = 56 * 1024 * 1024
BF = jnp.bfloat16
F32 = jnp.float32


def fit(fn, top, degree):
    cheb = np.polynomial.chebyshev.Chebyshev.interpolate(fn, degree, domain=[0.0, top])
    return [float(c) for c in cheb.convert(kind=np.polynomial.Polynomial).coef]


def root_cos(w):
    return np.cos(np.sqrt(np.maximum(w, 0.0)))


def root_sinc(w):
    return np.sinc(np.sqrt(np.maximum(w, 0.0)) / np.pi)


COS_WIDE = fit(root_cos, 10.0, 7)
SINC_WIDE = fit(root_sinc, 10.0, 6)
COS_SLIM = fit(root_cos, 1.6, 4)
SINC_SLIM = fit(root_sinc, 1.6, 4)


def horner(coefs, x):
    acc = jnp.full_like(x, coefs[-1])
    for c in coefs[-2::-1]:
        acc = acc * x + c
    return acc


def fourier_tables(extent):
    inner = extent // RADIX
    k = np.arange(RADIX)[:, None, None]
    q = np.arange(inner)[None, :, None]
    b = np.arange(inner)[None, None, :]
    angle = 2.0 * np.pi / extent * ((b * (k + RADIX * q)) % extent)
    cosine = np.cos(angle) / math.sqrt(extent)
    sine = np.sin(angle) / math.sqrt(extent)
    top = np.concatenate([cosine, sine], axis=2)
    low = np.concatenate([-sine, cosine], axis=2)
    table = np.concatenate([top, low], axis=1).astype(np.float32)
    return table.astype(BF), np.ascontiguousarray(table.transpose(0, 2, 1)).astype(BF)


def radix8(parts, sign):
    def add(x, y):
        return (x[0] + y[0], x[1] + y[1])

    def sub(x, y):
        return (x[0] - y[0], x[1] - y[1])

    def turn(x):
        return (x[1], -x[0]) if sign < 0 else (-x[1], x[0])

    half = math.sqrt(0.5)

    def four(x0, x1, x2, x3):
        t0, t1, t2, t3 = add(x0, x2), sub(x0, x2), add(x1, x3), turn(sub(x1, x3))
        return [add(t0, t2), add(t1, t3), sub(t0, t2), sub(t1, t3)]

    even = four(parts[0], parts[2], parts[4], parts[6])
    odd = four(parts[1], parts[3], parts[5], parts[7])
    turned1 = turn(odd[1])
    turned3 = turn(odd[3])
    odd[1] = ((odd[1][0] + turned1[0]) * half, (odd[1][1] + turned1[1]) * half)
    odd[2] = turn(odd[2])
    odd[3] = ((turned3[0] - odd[3][0]) * half, (turned3[1] - odd[3][1]) * half)
    return [add(even[i], odd[i]) for i in range(4)] + [sub(even[i], odd[i]) for i in range(4)]


def rows_of(step):
    return pl.ds(pl.multiple_of(step * SUB, SUB), SUB)


def residue(cut, shift, chunk, cuts, per):
    return lax.rem(cut + (cuts - shift), cuts) * per + chunk


def lines_kernel(cuts, cut_ref, p_ref, ft_ref, *rest):
    outs, y1 = rest[:-1], rest[-1]
    rows, extent = p_ref.shape[1], p_ref.shape[2]
    inner = extent // RADIX
    per = RADIX // cuts

    @pl.loop(0, rows // SUB)
    def _(step):
        at = rows_of(step)
        for l in range(0, inner, LANE):
            parts = [
                (
                    p_ref[0, at, a * inner + l : a * inner + l + LANE].astype(F32),
                    p_ref[1, at, a * inner + l : a * inner + l + LANE].astype(F32),
                )
                for a in range(RADIX)
            ]
            for k, (re, im) in enumerate(radix8(parts, -1)):
                y1[k, at, l : l + LANE] = re.astype(BF)
                y1[k, at, inner + l : inner + l + LANE] = im.astype(BF)

    cut = cut_ref[0]
    for s in range(cuts):
        for c in range(per):
            k = residue(cut, s, c, cuts, per)
            outs[s * per + c][...] = jnp.dot(y1[k], ft_ref[k], preferred_element_type=F32).astype(BF)


def across_kernel(cuts, *refs):
    pieces = refs[:cuts]
    f_ref, ft_ref, wx_ref, wy_ref = refs[cuts : cuts + 4]
    outs = refs[cuts + 4 : -3]
    y1, z, kb = refs[-3:]
    rows = pieces[0].shape[0]
    inner = rows * cuts // RADIX
    width = pieces[0].shape[1] // 2

    @pl.loop(0, inner // SUB)
    def _(step):
        for l in range(0, width, LANE):
            parts = []
            for a in range(RADIX):
                piece = pieces[a * inner // rows]
                at = pl.ds(pl.multiple_of(a * inner % rows + step * SUB, SUB), SUB)
                parts.append(
                    (
                        piece[at, l : l + LANE].astype(F32),
                        piece[at, width + l : width + l + LANE].astype(F32),
                    )
                )
            low = pl.ds(pl.multiple_of(step * SUB, SUB), SUB)
            high = pl.ds(pl.multiple_of(inner + step * SUB, SUB), SUB)
            for k, (re, im) in enumerate(radix8(parts, -1)):
                y1[k, low, l : l + LANE] = re.astype(BF)
                y1[k, high, l : l + LANE] = im.astype(BF)

    @pl.loop(0, RADIX)
    def _(k):
        z[...] = jnp.dot(f_ref[k], y1[k], preferred_element_type=F32)

        @pl.loop(0, inner // SUB)
        def _(step):
            low = pl.ds(pl.multiple_of(step * SUB, SUB), SUB)
            high = pl.ds(pl.multiple_of(inner + step * SUB, SUB), SUB)
            w = wx_ref[k, low, :] - wy_ref[...]
            size = jnp.abs(w)
            root = size * lax.rsqrt(jnp.maximum(size, 1e-30))
            onward = w > 0
            re = jnp.where(onward, horner(COS_WIDE, w), jnp.exp(-root))
            im = jnp.where(onward, root * horner(SINC_WIDE, w), 0.0)
            zr, zi = z[low, :], z[high, :]
            kb[low, :] = (zr * re - zi * im).astype(BF)
            kb[high, :] = (zr * im + zi * re).astype(BF)

        y1[k] = jnp.dot(ft_ref[k], kb[...], preferred_element_type=F32).astype(BF)

    @pl.loop(0, inner // SUB)
    def _(step):
        low = pl.ds(pl.multiple_of(step * SUB, SUB), SUB)
        high = pl.ds(pl.multiple_of(inner + step * SUB, SUB), SUB)
        for l in range(0, width, LANE):
            parts = [
                (y1[k, low, l : l + LANE].astype(F32), y1[k, high, l : l + LANE].astype(F32))
                for k in range(RADIX)
            ]
            for a, (re, im) in enumerate(radix8(parts, 1)):
                out = outs[a * inner // rows]
                at = pl.ds(pl.multiple_of(a * inner % rows + step * SUB, SUB), SUB)
                out[at, l : l + LANE] = re.astype(BF)
                out[at, width + l : width + l + LANE] = im.astype(BF)


def band_kernel(g_ref, off_ref, out_ref):
    rows, lanes = g_ref.shape[1], g_ref.shape[2]
    width = out_ref.shape[3]
    offset = off_ref[...]
    for part in range(2):
        x = jnp.concatenate(
            [g_ref[part].astype(F32), jnp.zeros((rows, width - lanes), F32)], axis=1
        )
        bit = 1
        while bit < width:
            x = jnp.where((offset & bit) != 0, pltpu.roll(x, bit, 1), x)
            bit *= 2
        out_ref[part, 0] = x.astype(BF)


def finish_kernel(cuts, split, cut_ref, num_ref, *refs):
    pieces = refs[:RADIX]
    f_ref, slow_in, band_ref, dx_ref, dy_ref, out_ref, z1, u, cr, ci = refs[RADIX:]
    rows, extent = slow_in.shape
    inner = extent // RADIX
    per = RADIX // cuts
    cut = cut_ref[0]
    scale = num_ref[0]
    turns = num_ref[1]
    share = num_ref[2]
    for s in range(cuts):
        for c in range(per):
            k = residue(cut, s, c, cuts, per)
            z1[k] = jnp.dot(
                pieces[s * per + c][...], f_ref[k], preferred_element_type=F32
            ).astype(BF)
    u[:, :, :PAD] = jnp.zeros((2, rows, PAD), BF)
    u[:, :, PAD + extent :] = jnp.zeros((2, rows, PAD), BF)

    @pl.loop(0, rows // SUB)
    def _(step):
        at = rows_of(step)
        for l in range(0, inner, LANE):
            parts = [
                (
                    z1[k, at, l : l + LANE].astype(F32),
                    z1[k, at, inner + l : inner + l + LANE].astype(F32),
                )
                for k in range(RADIX)
            ]
            for a, (re, im) in enumerate(radix8(parts, 1)):
                at_y = a * inner + l
                theta = scale * (slow_in[at, at_y : at_y + LANE].astype(F32) - slow_ref)
                square = theta * theta
                cosine = horner(COS_SLIM, square)
                sine = theta * horner(SINC_SLIM, square)
                u[0, at, PAD + at_y : PAD + at_y + LANE] = (re * cosine - im * sine).astype(BF)
                u[1, at, PAD + at_y : PAD + at_y + LANE] = (re * sine + im * cosine).astype(BF)

    contract = (((1,), (1,)), ((), ()))

    def mul(x, y):
        return lax.dot_general(x, y, contract, preferred_element_type=F32)

    for t in range(RADIX):
        wr = u[0, :, t * inner : t * inner + inner + 2 * PAD]
        wi = u[1, :, t * inner : t * inner + inner + 2 * PAD]
        cr[...] = mul(wr, band_ref[0, t]) - mul(wi, band_ref[1, t])
        ci[...] = mul(wr, band_ref[1, t]) + mul(wi, band_ref[0, t])

        @pl.loop(0, rows // SUB)
        def _(step):
            at = rows_of(step)
            first = t * inner
            vr = u[0, at, PAD + first : PAD + first + inner].astype(F32) + cr[at, :]
            vi = u[1, at, PAD + first : PAD + first + inner].astype(F32) + ci[at, :]
            distance = jnp.sqrt(dx_ref[at, :] + dy_ref[:, first : first + inner])
            turn = turns * distance
            theta = (turn - jnp.floor(turn + 0.5)) * (2.0 * math.pi)
            square = theta * theta
            value = (
                vr * horner(COS_WIDE, square) - vi * (theta * horner(SINC_WIDE, square))
            ) * share
            if split:
                size = out_ref.shape[2]
                for e in range(0, inner, size):
                    out_ref[(first + e) // size, at, :] = value[:, e : e + size]
            else:
                out_ref[at, first : first + inner] = value


def params():
    return pltpu.CompilerParams(vmem_limit_bytes=VMEM_LIMIT)


VMEM = pl.BlockSpec(memory_space=pltpu.VMEM)
SMEM = pl.BlockSpec(memory_space=pltpu.SMEM)


def lines_forward(field, ft, cut, cuts):
    rows, extent = field.shape[1], field.shape[2]
    inner = extent // RADIX
    tile = math.gcd(rows, 256)
    return pl.pallas_call(
        functools.partial(lines_kernel, cuts),
        grid=(rows // tile,),
        out_shape=[jax.ShapeDtypeStruct((rows, 2 * inner), BF)] * RADIX,
        in_specs=[
            SMEM,
            pl.BlockSpec((2, tile, extent), lambda i: (0, i, 0)),
            pl.BlockSpec(ft.shape, lambda i: (0, 0, 0)),
        ],
        out_specs=[pl.BlockSpec((tile, 2 * inner), lambda i: (i, 0))] * RADIX,
        scratch_shapes=[pltpu.VMEM((RADIX, tile, 2 * inner), BF)],
        compiler_params=params(),
        cost_estimate=pl.CostEstimate(
            flops=rows * RADIX * (2 * inner) ** 2 * 2,
            bytes_accessed=rows * extent * 8 + ft.size * 2,
            transcendentals=0,
        ),
        name="lines_forward",
    )(cut, field, ft)


def across(pieces, f, ft, wx, wy, cuts):
    rows = pieces[0].shape[0]
    inner = rows * cuts // RADIX
    width = pieces[0].shape[1] // 2
    return pl.pallas_call(
        functools.partial(across_kernel, cuts),
        out_shape=[jax.ShapeDtypeStruct((rows, 2 * width), BF)] * cuts,
        in_specs=[VMEM] * (cuts + 4),
        out_specs=[VMEM] * cuts,
        scratch_shapes=[
            pltpu.VMEM((RADIX, 2 * inner, width), BF),
            pltpu.VMEM((2 * inner, width), F32),
            pltpu.VMEM((2 * inner, width), BF),
        ],
        compiler_params=params(),
        cost_estimate=pl.CostEstimate(
            flops=2 * width * RADIX * (2 * inner) ** 2 * 2,
            bytes_accessed=24 * 1024 * 1024,
            transcendentals=0,
        ),
        name="across",
    )(*pieces, f, ft, wx, wy)


def band(rows_g, offsets, inner):
    extent = rows_g.shape[1]
    return pl.pallas_call(
        band_kernel,
        grid=(RADIX,),
        out_shape=jax.ShapeDtypeStruct((2, RADIX, inner, inner + 2 * PAD), BF),
        in_specs=[
            pl.BlockSpec((2, inner, rows_g.shape[2]), lambda t: (0, t, 0)),
            pl.BlockSpec((inner, 1), lambda t: (t, 0)),
        ],
        out_specs=pl.BlockSpec((2, 1, inner, inner + 2 * PAD), lambda t: (0, t, 0, 0)),
        compiler_params=params(),
        cost_estimate=pl.CostEstimate(
            flops=0, bytes_accessed=40 * 1024 * 1024, transcendentals=0
        ),
        name="band",
    )(rows_g, offsets)


def finish(pieces, chunk, chunks, f, slab, bands, dx, dy, cut, numbers, cuts, freqs):
    rows = pieces[0].shape[0] // chunks
    extent = slab.shape[1]
    inner = extent // RADIX
    size = extent // freqs
    split = size % LANE == 0 and inner % size == 0
    tile = math.gcd(rows, 128)
    steps = rows // tile
    if split:
        out_shape = jax.ShapeDtypeStruct((freqs, rows, size), F32)
        out_spec = pl.BlockSpec((freqs, tile, size), lambda i: (0, i, 0))
    else:
        out_shape = jax.ShapeDtypeStruct((rows, extent), F32)
        out_spec = pl.BlockSpec((tile, extent), lambda i: (i, 0))
    return pl.pallas_call(
        functools.partial(finish_kernel, cuts, split),
        grid=(steps,),
        out_shape=out_shape,
        in_specs=[SMEM, SMEM]
        + [pl.BlockSpec((tile, 2 * inner), lambda i: (i + chunk * steps, 0))] * RADIX
        + [
            pl.BlockSpec(f.shape, lambda i: (0, 0, 0)),
            pl.BlockSpec((tile, extent), lambda i: (i + chunk * steps, 0)),
            pl.BlockSpec(bands.shape, lambda i: (0, 0, 0, 0)),
            pl.BlockSpec((tile, 1), lambda i: (i + chunk * steps, 0)),
            pl.BlockSpec((1, extent), lambda i: (0, 0)),
        ],
        out_specs=out_spec,
        scratch_shapes=[
            pltpu.VMEM((RADIX, tile, 2 * inner), BF),
            pltpu.VMEM((2, tile, extent + 2 * PAD), BF),
            pltpu.VMEM((tile, inner), F32),
            pltpu.VMEM((tile, inner), F32),
        ],
        compiler_params=params(),
        cost_estimate=pl.CostEstimate(
            flops=rows * RADIX * (2 * inner) ** 2 * 6,
            bytes_accessed=32 * 1024 * 1024,
            transcendentals=0,
        ),
        name="finish",
    )(cut, numbers, *pieces, f, slab, bands, dx, dy), split


def wave_numbers(indices, extent):
    signed = jnp.where(indices < extent // 2, indices, indices - extent)
    return signed.astype(F32) * (2.0 * math.pi / (extent * grid_step))


def back(x, axis, shift):
    count = lax.axis_size(axis)
    return lax.ppermute(x, axis, [(i, (i - shift) % count) for i in range(count)])


def forth(x, axis, shift):
    count = lax.axis_size(axis)
    return lax.ppermute(x, axis, [(i, (i + shift) % count) for i in range(count)])


def body(wavefield, slowness, block_inverse, block_lengths, slab_owner, shot_position):
    cuts = lax.axis_size("cuts")
    freqs = lax.axis_size("freq")
    rows, extent_y = wavefield.shape[2], wavefield.shape[3]
    extent_x = rows * cuts
    inner_x, inner_y = extent_x // RADIX, extent_y // RADIX
    per = RADIX // cuts
    freq_index = lax.axis_index("freq")
    cut_index = lax.axis_index("cuts")
    cut = jnp.reshape(cut_index, (1,)).astype(jnp.int32)
    hertz = band_low + band_width * (freq_index.astype(F32) + 0.5) / freqs
    angular = 2.0 * math.pi * hertz

    fy, fty = fourier_tables(extent_y)
    fy, fty = jnp.asarray(fy), jnp.asarray(fty)
    if extent_x == extent_y:
        fx, ftx = fy, fty
    else:
        fx, ftx = fourier_tables(extent_x)
        fx, ftx = jnp.asarray(fx), jnp.asarray(ftx)

    owner = slab_owner[0]
    mine = freq_index == owner
    operators = lax.psum(jnp.where(mine, block_inverse[0], jnp.zeros_like(block_inverse[0])), "freq")
    slab = lax.psum(jnp.where(mine, slowness[0], jnp.zeros_like(slowness[0])), "freq")

    spectrum = lines_forward(wavefield[0], fty, cut, cuts)

    count_x = jnp.arange(RADIX, dtype=jnp.int32)[:, None] + RADIX * jnp.arange(inner_x, dtype=jnp.int32)[None, :]
    wx = (depth_step * depth_step) * (
        (angular * slow_ref) ** 2 - wave_numbers(count_x, extent_x) ** 2
    )
    wx = wx[:, :, None]
    received = [[None] * cuts for _ in range(per)]
    for c in range(per):
        received[c][0] = spectrum[c]
        for s in range(1, cuts):
            received[c][s] = back(spectrum[s * per + c], "cuts", s)
    results = []
    for c in range(per):
        line = cut_index * per + c + RADIX * jnp.arange(inner_y, dtype=jnp.int32)
        wy = ((depth_step * depth_step) * wave_numbers(line, extent_y) ** 2)[None, :]
        results.append(across(received[c], fx, ftx, wx, wy, cuts))

    operators, slab, _ = lax.optimization_barrier((operators, slab, results[-1][0]))
    whole = [operators]
    for s in range(1, cuts):
        whole.append(back(operators, "cuts", s))
    stacked = jnp.stack(whole)
    stacked = jnp.take(stacked, (jnp.arange(cuts) - cut_index) % cuts, axis=0)
    capacity = stacked.shape[-1]
    blocks = stacked.shape[2] * cuts
    matrices = jnp.moveaxis(stacked, 0, 1).reshape(2, blocks * capacity, capacity)
    lengths = lax.dynamic_index_in_dim(block_lengths, owner, 0, keepdims=False)
    ends = jnp.cumsum(lengths)
    starts = ends - lengths
    cells = jnp.arange(extent_y, dtype=jnp.int32)
    which = jnp.sum((ends[None, :] <= cells[:, None]).astype(jnp.int32), axis=1)
    chosen = which[:, None] == jnp.arange(blocks, dtype=jnp.int32)[None, :]
    start = jnp.sum(jnp.where(chosen, starts[None, :], 0), axis=1)
    length = jnp.sum(jnp.where(chosen, lengths[None, :], 0), axis=1)
    slot = which * capacity + cells - start
    picked = jnp.take(matrices, slot, axis=1)
    picked = jnp.where(
        jnp.arange(capacity, dtype=jnp.int32)[None, None, :] < length[None, :, None], picked, 0
    ).astype(BF)
    picked = jnp.pad(picked, ((0, 0), (0, 0), (0, -capacity % LANE)))
    offsets = start - (cells // inner_y * inner_y - PAD)
    bands = band(picked, offsets[:, None].astype(jnp.int32), inner_y)

    rows_x = cut_index * rows + jnp.arange(rows, dtype=jnp.int32)
    dx = (((rows_x - shot_position[0]).astype(F32) * grid_step) ** 2)[:, None]
    dy = (((cells - shot_position[1]).astype(F32) * grid_step) ** 2 + depth_step * depth_step)[None, :]
    numbers = jnp.stack(
        [angular * depth_step, hertz * slow_ref, jnp.asarray(1.0 / math.sqrt(freqs), F32)]
    )

    chunks = 2
    pieces = []
    for s in range(cuts):
        for c in range(per):
            pieces.append(results[c][s] if s == 0 else forth(results[c][s], "cuts", s))
    images = []
    for h in range(chunks):
        part, split = finish(pieces, h, chunks, fy, slab, bands, dx, dy, cut, numbers, cuts, freqs)
        if split:
            part = lax.psum_scatter(part, "freq", scatter_dimension=0, tiled=False)
        else:
            part = lax.psum_scatter(part, "freq", scatter_dimension=1, tiled=True)
        images.append(part)
    return jnp.concatenate(images, axis=0)[None]


def solution(mesh):
    placed = (
        P("freq", None, "cuts", None),
        P("freq", "cuts", None),
        P("freq", None, "cuts", None, None),
        P(),
        P(),
        P(),
    )
    return jax.shard_map(
        body, mesh=mesh, in_specs=placed, out_specs=P(None, "cuts", "freq"), check_vma=False
    )
```
